32 devices in a mesh: dp: 4 (over z), mp: 8 (over y, x, core).
Axes of the slice: x: 2, y: 2, z: 4, core: 2. Of those that a mesh axis runs over, the one named last changes fastest.
Arguments:
- tokens: bfloat16 [128, 4096], P(('dp', 'mp')), may hold values from -6 to 6
- hidden_grad: bfloat16 [128, 14336], P('dp', 'mp'), may hold values from -0.5 to 0.5
- gate_weight: bfloat16 [4096, 14336], P('dp', 'mp'), may hold values from -0.09375 to 0.09375
- up_weight: bfloat16 [4096, 14336], P('dp', 'mp'), may hold values from -0.09375 to 0.09375
- gate_probe: bfloat16 [4096, 14336], P('dp', 'mp'), may hold values from -1 to 1, as said below
- gate_mean: float32 [4096, 14336], P('dp', 'mp'), may hold values from -0.6 to 0.6
- gate_curve: float32 [4096, 14336], P('dp', 'mp'), may hold values from 1 to 10
- group_counts: int32 [4], replicated, may hold values from 8 to 32, as said below
Outputs:
- gate_weight_new: bfloat16 [4096, 14336], P('dp', 'mp')
- gate_mean_new: float32 [4096, 14336], P('dp', 'mp')
- gate_curve_new: float32 [4096, 14336], P('dp', 'mp')
The draws below stay inside these ranges and needn't reach their ends.
Inputs may be any that keep to these rules, and one draw needn't show every extreme that they name: `group_counts`: some data group has exactly 32 live tokens in every draw. `gate_probe`: every entry is -1 or 1, each sign drawn independently.
All inputs are finite; a program needn't handle non-finite values.
Results may differ from the reference program's by a relative error of at most 0.0017.
Values may be sent and summed in bfloat16 or wider, within the bound.
A program may use at most 128 MiB of HBM per device.

```python
import math
import jax
import jax.numpy as jnp
from jax import lax

D = 4096
FF = 14336
GROUP_ROWS = 32
TOKENS = 128
N_DP = 4


def draw_group_counts(key, part):
    first_key = jax.random.fold_in(key, 11)
    second_key = jax.random.fold_in(key, 12)
    least_rows = max(GROUP_ROWS // 4, 1)
    counts = jax.random.randint(first_key, (N_DP,), least_rows, GROUP_ROWS + 1, dtype=jnp.int32)
    chosen = jax.random.randint(second_key, (), 0, N_DP, dtype=jnp.int32)
    positions = jnp.arange(N_DP, dtype=jnp.int32)
    return jnp.where(positions == chosen, GROUP_ROWS, counts).astype(jnp.int32)


def draw_gate_probe(key, part):
    sign_key = jax.random.fold_in(key, 21)
    signs = jax.random.randint(sign_key, (D, FF), 0, 2, dtype=jnp.int32)
    values = 2.0 * signs.astype(jnp.float32) - 1.0
    return values.astype(jnp.bfloat16)


def block_levels(own_key, dims, shards, least, largest):
    level, own = 1.0, jax.random.fold_in(own_key, 6)
    for dim, blocks in shards:
        steps = jnp.exp(jax.random.uniform(jax.random.fold_in(own, dim), (blocks,), jnp.float32, least / len(shards), largest / len(shards)))
        level = level * jnp.repeat(steps, dims[dim] // blocks).reshape([-1 if axis == dim else 1 for axis in range(len(dims))])
    return level


def normal_values(key, shape, scale, bound, split=(), kind=jnp.bfloat16):
    drawn = scale * jax.random.normal(key, shape, jnp.float32)
    if split:
        drawn = drawn * block_levels(key, shape, split, -0.22, 0.18)
    return jnp.clip(drawn, -bound, bound).astype(kind)


def setup_inputs(seed: int = 0) -> dict:
    key_list = jax.random.split(jax.random.key(seed), 9)
    return {
        "tokens": normal_values(key_list[0], (TOKENS, D), 1.0, 6.0, ((0, 32),)),
        "hidden_grad": normal_values(key_list[1], (TOKENS, FF), TOKENS ** -0.5, 0.5, ((0, 4), (1, 8))),
        "gate_weight": normal_values(key_list[2], (D, FF), D ** -0.5, 0.09375, ((0, 4), (1, 8))),
        "up_weight": normal_values(key_list[3], (D, FF), D ** -0.5, 0.09375, ((0, 4), (1, 8))),
        "gate_probe": draw_gate_probe(jax.random.fold_in(key_list[8], 71), 0),
        "gate_mean": normal_values(key_list[5], (D, FF), 0.1, 0.6, ((0, 4), (1, 8)), jnp.float32),
        "gate_curve": jnp.clip(jnp.exp(math.log(10.0) - 2.3025851 * jax.random.uniform(key_list[6], (D, FF), jnp.float32) ** block_levels(key_list[6], (D, FF), ((0, 4), (1, 8)), -0.2, 0.2)), 1.0, 10.0),
        "group_counts": draw_group_counts(jax.random.fold_in(key_list[8], 71), 0),
    }


first_decay = 0.9
second_decay = 0.999
learn_rate = 0.15
epsilon_term = 0.0001
first_fix = 1.0 - 0.9 ** 10
second_fix = 1.0 - 0.999 ** 10

def silu_parts(inputs):
    sigmoid_part = jax.nn.sigmoid(inputs)
    silu_slope = sigmoid_part * (1.0 + inputs * (1.0 - sigmoid_part))
    silu_bend = sigmoid_part * (1.0 - sigmoid_part) * (2.0 + inputs * (1.0 - 2.0 * sigmoid_part))
    return (silu_slope, silu_bend)

def adahessian(weight, mean_old, curve_old, gradient, probe_value, product):
    diagonal = probe_value.astype(jnp.float32) * product
    mean_new = first_decay * mean_old + (1.0 - first_decay) * gradient
    curve_new = second_decay * curve_old + (1.0 - second_decay) * diagonal * diagonal
    step_ratio = mean_new / first_fix / (jnp.sqrt(curve_new / second_fix) + epsilon_term)
    weight_new = (weight.astype(jnp.float32) - learn_rate * step_ratio).astype(jnp.bfloat16)
    return (weight_new, mean_new, curve_new)

def reference(tokens, hidden_grad, gate_weight, up_weight, gate_probe, gate_mean, gate_curve, group_counts):
    total_rows = tokens.shape[0]
    row_ids = jnp.arange(total_rows, dtype=jnp.int32)
    limits = jnp.repeat(group_counts.astype(jnp.int32), GROUP_ROWS, total_repeat_length=total_rows)
    live = (row_ids % GROUP_ROWS < limits).astype(jnp.float32)

    def project(weight):
        return jnp.dot(tokens, weight, preferred_element_type=jnp.float32)
    gate_pre = project(gate_weight)
    up_pre = project(up_weight)
    gate_tan = project(gate_probe)
    silu_slope, silu_bend = silu_parts(gate_pre)
    masked = hidden_grad.astype(jnp.float32) * live[:, None]
    grad_gate = (masked * up_pre * silu_slope).astype(jnp.bfloat16)
    tan_gate = (masked * up_pre * silu_bend * gate_tan).astype(jnp.bfloat16)

    def contract(rows):
        return lax.dot_general(tokens, rows, (((0,), (0,)), ((), ())), preferred_element_type=jnp.float32)
    gate_gradient = contract(grad_gate)
    gate_hz = contract(tan_gate)
    gate_out = adahessian(gate_weight, gate_mean, gate_curve, gate_gradient, gate_probe, gate_hz)
    return (gate_out[0], gate_out[1], gate_out[2])
```

```python
import jax
import jax.numpy as jnp
from jax import lax
from jax.sharding import PartitionSpec as P

first_decay = 0.9
second_decay = 0.999
learn_rate = 0.15
epsilon_term = 0.0001
first_fix = 1.0 - 0.9**10
second_fix = 1.0 - 0.999**10


def silu_parts(inputs):
    sigmoid_part = jax.nn.sigmoid(inputs)
    silu_slope = sigmoid_part * (1.0 + inputs * (1.0 - sigmoid_part))
    silu_bend = sigmoid_part * (1.0 - sigmoid_part) * (2.0 + inputs * (1.0 - 2.0 * sigmoid_part))
    return (silu_slope, silu_bend)


def adahessian(weight, mean_old, curve_old, gradient, probe_value, product):
    diagonal = probe_value.astype(jnp.float32) * product
    mean_new = first_decay * mean_old + (1.0 - first_decay) * gradient
    curve_new = second_decay * curve_old + (1.0 - second_decay) * diagonal * diagonal
    step_ratio = mean_new / first_fix / (jnp.sqrt(curve_new / second_fix) + epsilon_term)
    weight_new = (weight.astype(jnp.float32) - learn_rate * step_ratio).astype(jnp.bfloat16)
    return (weight_new, mean_new, curve_new)


def body(
    tokens, hidden_grad, gate_weight, up_weight, gate_probe, gate_mean, gate_curve, group_counts
):
    shards = lax.axis_size("dp")
    local_rows, features = tokens.shape
    own = lax.all_to_all(tokens, "dp", split_axis=1, concat_axis=0, tiled=True)
    spread = lax.all_gather(own, "mp", axis=0)
    peers = spread.shape[0]
    depth = features // shards
    columns = spread.reshape(peers, shards, local_rows, depth)
    columns = columns.transpose(1, 0, 2, 3).reshape(-1, depth)
    group_rows = peers * local_rows
    width = gate_weight.shape[1]
    partial = jnp.concatenate(
        [
            jnp.dot(columns, piece, preferred_element_type=jnp.float32)
            for piece in (gate_weight, up_weight, gate_probe)
        ],
        axis=1,
    )
    total = lax.psum_scatter(partial, "dp", scatter_dimension=0, tiled=True)
    gate_pre, up_pre, gate_tan = (total[:, i * width : (i + 1) * width] for i in range(3))
    group_index = lax.axis_index("dp")
    limit = lax.dynamic_index_in_dim(group_counts, group_index, 0, keepdims=False)
    live = (jnp.arange(group_rows, dtype=jnp.int32) < limit).astype(jnp.float32)
    silu_slope, silu_bend = silu_parts(gate_pre)
    masked = hidden_grad.astype(jnp.float32) * live[:, None]
    grad_gate = (masked * up_pre * silu_slope).astype(jnp.bfloat16)
    tan_gate = (masked * up_pre * silu_bend * gate_tan).astype(jnp.bfloat16)
    packed = jnp.concatenate([grad_gate, tan_gate], 1)
    sums = lax.dot_general(
        columns,
        lax.all_gather(packed, "dp", axis=0, tiled=True),
        (((0,), (0,)), ((), ())),
        preferred_element_type=jnp.float32,
    )
    return adahessian(
        gate_weight, gate_mean, gate_curve, sums[:, :width], gate_probe, sums[:, width:]
    )


def solution(mesh):
    return jax.shard_map(
        body,
        mesh=mesh,
        in_specs=(
            P(("dp", "mp"), None),
            P("dp", "mp"),
            P("dp", "mp"),
            P("dp", "mp"),
            P("dp", "mp"),
            P("dp", "mp"),
            P("dp", "mp"),
            P(),
        ),
        out_specs=(P("dp", "mp"), P("dp", "mp"), P("dp", "mp")),
        check_vma=False,
    )
```

```python
import functools

import jax
import jax.numpy as jnp
from jax import lax
from jax.experimental import pallas as pl
from jax.experimental.pallas import tpu as pltpu
from jax.sharding import PartitionSpec as P

first_decay = 0.9
second_decay = 0.999
learn_rate = 0.15
epsilon_term = 0.0001
first_fix = 1.0 - 0.9**10
second_fix = 1.0 - 0.999**10


def silu_parts(inputs):
    sigmoid_part = jax.nn.sigmoid(inputs)
    silu_slope = sigmoid_part * (1.0 + inputs * (1.0 - sigmoid_part))
    silu_bend = sigmoid_part * (1.0 - sigmoid_part) * (2.0 + inputs * (1.0 - 2.0 * sigmoid_part))
    return (silu_slope, silu_bend)


def adahessian(weight, mean_old, curve_old, gradient, probe_value, product):
    diagonal = probe_value.astype(jnp.float32) * product
    mean_new = first_decay * mean_old + (1.0 - first_decay) * gradient
    curve_new = second_decay * curve_old + (1.0 - second_decay) * diagonal * diagonal
    step_ratio = mean_new / first_fix / (jnp.sqrt(curve_new / second_fix) + epsilon_term)
    weight_new = (weight.astype(jnp.float32) - learn_rate * step_ratio).astype(jnp.bfloat16)
    return (weight_new, mean_new, curve_new)


def plain_body(
    tokens, hidden_grad, gate_weight, up_weight, gate_probe, gate_mean, gate_curve, group_counts
):
    shards = lax.axis_size("dp")
    local_rows, features = tokens.shape
    own = lax.all_to_all(tokens, "dp", split_axis=1, concat_axis=0, tiled=True)
    spread = lax.all_gather(own, "mp", axis=0)
    peers = spread.shape[0]
    depth = features // shards
    columns = spread.reshape(peers, shards, local_rows, depth)
    columns = columns.transpose(1, 0, 2, 3).reshape(-1, depth)
    group_rows = peers * local_rows
    width = gate_weight.shape[1]
    partial = jnp.concatenate(
        [
            jnp.dot(columns, piece, preferred_element_type=jnp.float32)
            for piece in (gate_weight, up_weight, gate_probe)
        ],
        axis=1,
    )
    total = lax.psum_scatter(partial, "dp", scatter_dimension=0, tiled=True)
    gate_pre, up_pre, gate_tan = (total[:, i * width : (i + 1) * width] for i in range(3))
    group_index = lax.axis_index("dp")
    limit = lax.dynamic_index_in_dim(group_counts, group_index, 0, keepdims=False)
    live = (jnp.arange(group_rows, dtype=jnp.int32) < limit).astype(jnp.float32)
    silu_slope, silu_bend = silu_parts(gate_pre)
    masked = hidden_grad.astype(jnp.float32) * live[:, None]
    grad_gate = (masked * up_pre * silu_slope).astype(jnp.bfloat16)
    tan_gate = (masked * up_pre * silu_bend * gate_tan).astype(jnp.bfloat16)
    packed = jnp.concatenate([grad_gate, tan_gate], 1)
    sums = lax.dot_general(
        columns,
        lax.all_gather(packed, "dp", axis=0, tiled=True),
        (((0,), (0,)), ((), ())),
        preferred_element_type=jnp.float32,
    )
    return adahessian(
        gate_weight, gate_mean, gate_curve, sums[:, :width], gate_probe, sums[:, width:]
    )


CHUNK = 256
LAG = 2
BACK = 6


def exchange_kernel(
    shards, peers, tok_ref, grad_ref, gate_ref, up_ref, probe_ref, g_ref, colt_ref,
    w, s1, s2, cols, grad, pbuf, rbuf,
    wsem, s1_send, s1_recv, s2_send, s2_recv, h_send, h_recv, p_send, p_recv, g_send, g_recv,
):
    d = lax.axis_index("dp")
    m = lax.axis_index("mp")
    last = shards - 1
    features = tok_ref.shape[1]
    rows = tok_ref.shape[0]
    depth = features // shards
    width = gate_ref.shape[1]
    chunks = width // CHUNK
    total = rows * peers
    half = total // 2
    group = grad_ref.shape[0]

    loads = [
        pltpu.make_async_copy(ref, w.at[i], wsem.at[i])
        for i, ref in enumerate((gate_ref, up_ref, probe_ref))
    ]
    for load in loads:
        load.start()

    barrier = pltpu.get_barrier_semaphore()
    for k in range(1, shards):
        pl.semaphore_signal(
            barrier, inc=1, device_id=(lax.rem(d + k, shards), m),
            device_id_type=pl.DeviceIdType.MESH,
        )
    for k in range(1, peers):
        pl.semaphore_signal(
            barrier, inc=1, device_id=(d, lax.rem(m + k, peers)),
            device_id_type=pl.DeviceIdType.MESH,
        )
    pl.semaphore_wait(barrier, shards + peers - 2)

    def remote(src, dst, send, recv, device):
        return pltpu.make_async_remote_copy(
            src_ref=src, dst_ref=dst, send_sem=send, recv_sem=recv,
            device_id=device, device_id_type=pl.DeviceIdType.MESH,
        )

    first = []
    for k in range(1, shards):
        to = lax.rem(d + k, shards)
        first.append(
            remote(
                tok_ref.at[:, pl.ds(pl.multiple_of(to * depth, depth), depth)],
                s1.at[k - 1], s1_send.at[k - 1], s1_recv.at[k - 1], (to, m),
            )
        )
        first[-1].start()

    low = remote(grad_ref, grad.at[pl.ds(group, group)], h_send, h_recv, (0, m))
    high = remote(grad_ref, grad.at[pl.ds(0, group)], h_send, h_recv, (last, m))

    @pl.when(d == 1)
    def _():
        low.start()

    @pl.when(d == 2)
    def _():
        high.start()

    @pl.when(d == 0)
    def _():
        grad[pl.ds(0, group), :] = grad_ref[...]

    @pl.when(d == last)
    def _():
        grad[pl.ds(group, group), :] = grad_ref[...]

    joined = tok_ref[:, pl.ds(pl.multiple_of(d * depth, depth), depth)].astype(jnp.float32)
    for k in range(1, shards):
        first[k - 1].wait_recv()
        joined = joined + s1[k - 1].astype(jnp.float32)
    s2[m] = joined.astype(jnp.bfloat16)
    second = []
    for k in range(1, peers):
        second.append(
            remote(
                s2.at[m], s2.at[m], s2_send.at[k - 1], s2_recv.at[k - 1],
                (d, lax.rem(m + k, peers)),
            )
        )
        second[-1].start()
    for copy in second:
        copy.wait_recv()

    local = rows // shards
    target = lax.broadcasted_iota(jnp.int32, (total, total), 0)
    source = lax.broadcasted_iota(jnp.int32, (total, total), 1)
    t_group = target // group
    t_rest = target - t_group * group
    t_peer = t_rest // local
    wanted = t_peer * rows + t_group * local + (t_rest - t_peer * local)
    order = jnp.where(wanted == source, 1.0, 0.0).astype(jnp.bfloat16)
    sorted_rows = jnp.dot(
        order, s2[...].reshape(total, depth), preferred_element_type=jnp.float32
    )
    cols[...] = sorted_rows.astype(jnp.bfloat16)
    colt_ref[...] = sorted_rows.T.astype(jnp.bfloat16)
    for load in loads:
        load.wait()

    places = (last - d, d)
    nexts = (jnp.maximum(d - 1, 0), jnp.minimum(d + 1, last))
    prevs = (jnp.minimum(d + 1, last), jnp.maximum(d - 1, 0))

    def forward(c, side):
        return remote(
            pbuf.at[c, side], rbuf.at[c, side], p_send.at[c, side], p_recv.at[c, side],
            (nexts[side], m),
        )

    def backward(c, side):
        part = g_ref.at[c, pl.ds(side * half, half)]
        return remote(part, part, g_send.at[c, side], g_recv.at[c, side], (prevs[side], m))

    def multiply(c):
        where = pl.ds(pl.multiple_of(c * CHUNK, CHUNK), CHUNK)
        for i in range(3):
            product = jnp.dot(cols[...], w[i, :, where], preferred_element_type=jnp.float32)
            for side in range(2):
                pbuf[c, side, :, pl.ds(i * CHUNK, CHUNK)] = product[side * half : (side + 1) * half]
        for side in range(2):

            @pl.when(places[side] == 0)
            def _():
                forward(c, side).start()

    def relay(c):
        where = pl.ds(pl.multiple_of(c * CHUNK, CHUNK), CHUNK)
        for side in range(2):

            @pl.when(places[side] > 0)
            def _():
                forward(c, side).wait_recv()

            @pl.when(jnp.logical_and(places[side] > 0, places[side] < last))
            def _():
                pbuf[c, side] = pbuf[c, side] + rbuf[c, side]
                forward(c, side).start()

            @pl.when(places[side] == last)
            def _():
                gate_pre, up_pre, gate_tan = (
                    pbuf[c, side, :, pl.ds(i * CHUNK, CHUNK)]
                    + rbuf[c, side, :, pl.ds(i * CHUNK, CHUNK)]
                    for i in range(3)
                )
                silu_slope, silu_bend = silu_parts(gate_pre)
                scaled = grad[:, where].astype(jnp.float32) * up_pre
                g_ref[c, pl.ds(side * half, half), pl.ds(0, CHUNK)] = (
                    scaled * silu_slope
                ).astype(jnp.bfloat16)
                g_ref[c, pl.ds(side * half, half), pl.ds(CHUNK, CHUNK)] = (
                    scaled * silu_bend * gate_tan
                ).astype(jnp.bfloat16)
                backward(c, side).start()

    def give_back(c):
        for side in range(2):

            @pl.when(places[side] < last)
            def _():
                backward(c, side).wait_recv()

            @pl.when(jnp.logical_and(places[side] > 0, places[side] < last))
            def _():
                backward(c, side).start()

    @pl.when(d == 0)
    def _():
        low.wait_recv()

    @pl.when(d == last)
    def _():
        high.wait_recv()

    def step(s, carry):
        @pl.when(s < chunks)
        def _():
            multiply(s)

        @pl.when(jnp.logical_and(s >= LAG, s < chunks + LAG))
        def _():
            relay(s - LAG)

        @pl.when(s >= BACK)
        def _():
            give_back(s - BACK)

        return carry

    lax.fori_loop(0, chunks + BACK, step, 0)

    def drain(c, carry):
        for side in range(2):

            @pl.when(places[side] < last)
            def _():
                forward(c, side).wait_send()

            @pl.when(places[side] > 0)
            def _():
                backward(c, side).wait_send()

        return carry

    lax.fori_loop(0, chunks, drain, 0)
    for copy in first + second:
        copy.wait_send()

    @pl.when(d == 1)
    def _():
        low.wait_send()

    @pl.when(d == 2)
    def _():
        high.wait_send()


def exchange(padded, grad, gate_weight, up_weight, gate_probe):
    shards, peers = lax.axis_size("dp"), lax.axis_size("mp")
    rows, features = padded.shape
    depth, width = gate_weight.shape
    chunks = width // CHUNK
    total = rows * peers
    half = total // 2
    vmem = pl.BlockSpec(memory_space=pltpu.VMEM)
    hbm = pl.BlockSpec(memory_space=pl.ANY)
    dma = pltpu.SemaphoreType.DMA
    return pl.pallas_call(
        functools.partial(exchange_kernel, shards, peers),
        out_shape=(
            jax.ShapeDtypeStruct((chunks, total, 2 * CHUNK), jnp.bfloat16),
            jax.ShapeDtypeStruct((depth, total), jnp.bfloat16),
        ),
        in_specs=[vmem, vmem, hbm, hbm, hbm],
        out_specs=(vmem, vmem),
        scratch_shapes=[
            pltpu.VMEM((3, depth, width), jnp.bfloat16),
            pltpu.VMEM((shards - 1, rows, depth), jnp.bfloat16),
            pltpu.VMEM((peers, rows, depth), jnp.bfloat16),
            pltpu.VMEM((total, depth), jnp.bfloat16),
            pltpu.VMEM((half, width), jnp.bfloat16),
            pltpu.VMEM((chunks, 2, half, 3 * CHUNK), jnp.float32),
            pltpu.VMEM((chunks, 2, half, 3 * CHUNK), jnp.float32),
            dma((3,)),
            dma((shards - 1,)),
            dma((shards - 1,)),
            dma((peers - 1,)),
            dma((peers - 1,)),
            dma,
            dma,
            dma((chunks, 2)),
            dma((chunks, 2)),
            dma((chunks, 2)),
            dma((chunks, 2)),
        ],
        compiler_params=pltpu.CompilerParams(
            collective_id=0, has_side_effects=True, vmem_limit_bytes=40 << 20
        ),
    )(padded, grad, gate_weight, up_weight, gate_probe)


def update_kernel(
    colt_ref, g_ref, weight_ref, probe_ref, mean_ref, curve_ref, weight_out, mean_out, curve_out
):
    sums = jnp.dot(colt_ref[...], g_ref[0], preferred_element_type=jnp.float32)
    weight_out[...], mean_out[...], curve_out[...] = adahessian(
        weight_ref[...], mean_ref[...], curve_ref[...],
        sums[:, :CHUNK], probe_ref[...], sums[:, CHUNK:],
    )


UPDATE_ROWS = 512


def update(colt, g, weight, probe, mean, curve):
    depth, width = weight.shape
    total = colt.shape[1]
    block = pl.BlockSpec((UPDATE_ROWS, CHUNK), lambda i, j: (j, i))
    return pl.pallas_call(
        update_kernel,
        grid=(width // CHUNK, depth // UPDATE_ROWS),
        in_specs=[
            pl.BlockSpec((UPDATE_ROWS, total), lambda i, j: (j, 0)),
            pl.BlockSpec((1, total, 2 * CHUNK), lambda i, j: (i, 0, 0)),
            block, block, block, block,
        ],
        out_specs=(block, block, block),
        out_shape=(
            jax.ShapeDtypeStruct(weight.shape, weight.dtype),
            jax.ShapeDtypeStruct(mean.shape, mean.dtype),
            jax.ShapeDtypeStruct(curve.shape, curve.dtype),
        ),
        compiler_params=pltpu.CompilerParams(vmem_limit_bytes=32 << 20),
    )(colt, g, weight, probe, mean, curve)


def body(
    tokens, hidden_grad, gate_weight, up_weight, gate_probe, gate_mean, gate_curve, group_counts
):
    shards = lax.axis_size("dp")
    local, depth, width = tokens.shape[0], gate_weight.shape[0], gate_weight.shape[1]
    fits = shards == 4 and (shards * local) % 16 == 0 and hidden_grad.shape[0] % 16 == 0
    if not (fits and width % CHUNK == 0 and depth % UPDATE_ROWS == 0 and width <= 2048):
        return plain_body(
            tokens, hidden_grad, gate_weight, up_weight, gate_probe,
            gate_mean, gate_curve, group_counts,
        )
    d = lax.axis_index("dp")
    limit = lax.dynamic_index_in_dim(group_counts, d, 0, keepdims=False)
    live = jnp.arange(hidden_grad.shape[0], dtype=jnp.int32) < limit
    grad = jnp.where(live[:, None], hidden_grad, jnp.zeros_like(hidden_grad))
    slot = jnp.arange(shards * local, dtype=jnp.int32) // local
    repeated = jnp.tile(tokens, (shards, 1))
    padded = jnp.where((slot == d)[:, None], repeated, jnp.zeros_like(repeated))
    g, colt = exchange(padded, grad, gate_weight, up_weight, gate_probe)
    return update(colt, g, gate_weight, gate_probe, gate_mean, gate_curve)


def solution(mesh):
    return jax.shard_map(
        body,
        mesh=mesh,
        in_specs=(
            P(("dp", "mp"), None),
            P("dp", "mp"),
            P("dp", "mp"),
            P("dp", "mp"),
            P("dp", "mp"),
            P("dp", "mp"),
            P("dp", "mp"),
            P(),
        ),
        out_specs=(P("dp", "mp"), P("dp", "mp"), P("dp", "mp")),
        check_vma=False,
    )
```

```python
import functools

import jax
import jax.numpy as jnp
from jax import lax
from jax.experimental import pallas as pl
from jax.experimental.pallas import tpu as pltpu
from jax.sharding import PartitionSpec as P

first_decay = 0.9
second_decay = 0.999
learn_rate = 0.15
epsilon_term = 0.0001
first_fix = 1.0 - 0.9**10
second_fix = 1.0 - 0.999**10


def silu_parts(inputs):
    sigmoid_part = jax.nn.sigmoid(inputs)
    silu_slope = sigmoid_part * (1.0 + inputs * (1.0 - sigmoid_part))
    silu_bend = sigmoid_part * (1.0 - sigmoid_part) * (2.0 + inputs * (1.0 - 2.0 * sigmoid_part))
    return (silu_slope, silu_bend)


def adahessian(weight, mean_old, curve_old, gradient, probe_value, product):
    diagonal = probe_value.astype(jnp.float32) * product
    mean_new = first_decay * mean_old + (1.0 - first_decay) * gradient
    curve_new = second_decay * curve_old + (1.0 - second_decay) * diagonal * diagonal
    step_ratio = mean_new / first_fix / (jnp.sqrt(curve_new / second_fix) + epsilon_term)
    weight_new = (weight.astype(jnp.float32) - learn_rate * step_ratio).astype(jnp.bfloat16)
    return (weight_new, mean_new, curve_new)


def plain_body(
    tokens, hidden_grad, gate_weight, up_weight, gate_probe, gate_mean, gate_curve, group_counts
):
    shards = lax.axis_size("dp")
    local_rows, features = tokens.shape
    own = lax.all_to_all(tokens, "dp", split_axis=1, concat_axis=0, tiled=True)
    spread = lax.all_gather(own, "mp", axis=0)
    peers = spread.shape[0]
    depth = features // shards
    columns = spread.reshape(peers, shards, local_rows, depth)
    columns = columns.transpose(1, 0, 2, 3).reshape(-1, depth)
    group_rows = peers * local_rows
    width = gate_weight.shape[1]
    partial = jnp.concatenate(
        [
            jnp.dot(columns, piece, preferred_element_type=jnp.float32)
            for piece in (gate_weight, up_weight, gate_probe)
        ],
        axis=1,
    )
    total = lax.psum_scatter(partial, "dp", scatter_dimension=0, tiled=True)
    gate_pre, up_pre, gate_tan = (total[:, i * width : (i + 1) * width] for i in range(3))
    group_index = lax.axis_index("dp")
    limit = lax.dynamic_index_in_dim(group_counts, group_index, 0, keepdims=False)
    live = (jnp.arange(group_rows, dtype=jnp.int32) < limit).astype(jnp.float32)
    silu_slope, silu_bend = silu_parts(gate_pre)
    masked = hidden_grad.astype(jnp.float32) * live[:, None]
    grad_gate = (masked * up_pre * silu_slope).astype(jnp.bfloat16)
    tan_gate = (masked * up_pre * silu_bend * gate_tan).astype(jnp.bfloat16)
    packed = jnp.concatenate([grad_gate, tan_gate], 1)
    sums = lax.dot_general(
        columns,
        lax.all_gather(packed, "dp", axis=0, tiled=True),
        (((0,), (0,)), ((), ())),
        preferred_element_type=jnp.float32,
    )
    return adahessian(
        gate_weight, gate_mean, gate_curve, sums[:, :width], gate_probe, sums[:, width:]
    )


CHUNK = 128
FLIGHT = 1
GROUPED = 2


def exchange_kernel(
    shards, peers, tok_ref, grad_ref, gate_ref, up_ref, probe_ref, g_ref, colt_ref,
    w, s1, s2, cols, grad, pbuf, rbuf,
    wsem, s1_send, s1_recv, s2_send, s2_recv, h_send, h_recv, p_send, p_recv, g_send, g_recv,
):
    d = lax.axis_index("dp")
    m = lax.axis_index("mp")
    last = shards - 1
    features = tok_ref.shape[1]
    rows = tok_ref.shape[0]
    depth = features // shards
    width = gate_ref.shape[1]
    chunks = width // CHUNK
    total = rows * peers
    half = total // 2
    group = grad_ref.shape[0]

    loads = [
        pltpu.make_async_copy(ref, w.at[i], wsem.at[i])
        for i, ref in enumerate((gate_ref, up_ref, probe_ref))
    ]
    for load in loads:
        load.start()

    barrier = pltpu.get_barrier_semaphore()
    for k in range(1, shards):
        pl.semaphore_signal(
            barrier, inc=1, device_id=(lax.rem(d + k, shards), m),
            device_id_type=pl.DeviceIdType.MESH,
        )
    for k in range(1, peers):
        pl.semaphore_signal(
            barrier, inc=1, device_id=(d, lax.rem(m + k, peers)),
            device_id_type=pl.DeviceIdType.MESH,
        )
    pl.semaphore_wait(barrier, shards + peers - 2)

    def remote(src, dst, send, recv, device):
        return pltpu.make_async_remote_copy(
            src_ref=src, dst_ref=dst, send_sem=send, recv_sem=recv,
            device_id=device, device_id_type=pl.DeviceIdType.MESH,
        )

    first = []
    for k in range(1, shards):
        to = lax.rem(d + k, shards)
        first.append(
            remote(
                tok_ref.at[:, pl.ds(pl.multiple_of(to * depth, depth), depth)],
                s1.at[k - 1], s1_send.at[k - 1], s1_recv.at[k - 1], (to, m),
            )
        )
        first[-1].start()

    low = remote(grad_ref, grad.at[pl.ds(group, group)], h_send, h_recv, (0, m))
    high = remote(grad_ref, grad.at[pl.ds(0, group)], h_send, h_recv, (last, m))

    @pl.when(d == 1)
    def _():
        low.start()

    @pl.when(d == 2)
    def _():
        high.start()

    @pl.when(d == 0)
    def _():
        grad[pl.ds(0, group), :] = grad_ref[...]

    @pl.when(d == last)
    def _():
        grad[pl.ds(group, group), :] = grad_ref[...]

    joined = tok_ref[:, pl.ds(pl.multiple_of(d * depth, depth), depth)].astype(jnp.float32)
    for k in range(1, shards):
        first[k - 1].wait_recv()
        joined = joined + s1[k - 1].astype(jnp.float32)
    s2[m] = joined.astype(jnp.bfloat16)
    second = []
    for k in range(1, peers):
        second.append(
            remote(
                s2.at[m], s2.at[m], s2_send.at[k - 1], s2_recv.at[k - 1],
                (d, lax.rem(m + k, peers)),
            )
        )
        second[-1].start()
    for copy in second:
        copy.wait_recv()

    local = rows // shards
    target = lax.broadcasted_iota(jnp.int32, (total, total), 0)
    source = lax.broadcasted_iota(jnp.int32, (total, total), 1)
    t_group = target // group
    t_rest = target - t_group * group
    t_peer = t_rest // local
    wanted = t_peer * rows + t_group * local + (t_rest - t_peer * local)
    order = jnp.where(wanted == source, 1.0, 0.0).astype(jnp.bfloat16)
    sorted_rows = jnp.dot(
        order, s2[...].reshape(total, depth), preferred_element_type=jnp.float32
    )
    cols[...] = sorted_rows.astype(jnp.bfloat16)
    colt_ref[...] = sorted_rows.T.astype(jnp.bfloat16)
    for load in loads:
        load.wait()

    places = (last - d, d)
    nexts = (jnp.maximum(d - 1, 0), jnp.minimum(d + 1, last))
    prevs = (jnp.minimum(d + 1, last), jnp.maximum(d - 1, 0))

    def forward(c, side):
        return remote(
            pbuf.at[c, side], rbuf.at[c, side], p_send.at[c, side], p_recv.at[c, side],
            (nexts[side], m),
        )

    def backward(c, side):
        part = g_ref.at[c, pl.ds(side * half, half)]
        return remote(part, part, g_send.at[c, side], g_recv.at[c, side], (prevs[side], m))

    def multiply(c):
        where = pl.ds(pl.multiple_of(c * CHUNK, CHUNK), CHUNK)
        for i in range(3):
            product = jnp.dot(cols[...], w[i, :, where], preferred_element_type=jnp.float32)
            for side in range(2):
                pbuf[c, side, :, pl.ds(i * CHUNK, CHUNK)] = product[side * half : (side + 1) * half]
        for side in range(2):

            @pl.when(jnp.logical_and(places[side] == 0, c >= FLIGHT))
            def _():
                forward(c - FLIGHT, side).wait_send()

            @pl.when(places[side] == 0)
            def _():
                forward(c, side).start()

    def relay(s):
        for side in range(2):
            c = s - places[side]
            inside = jnp.logical_and(c >= 0, c < chunks)

            @pl.when(inside)
            def _(c=c, side=side):
                relay_side(c, side)

    def relay_side(c, side):
        where = pl.ds(pl.multiple_of(c * CHUNK, CHUNK), CHUNK)

        @pl.when(places[side] > 0)
        def _():
            forward(c, side).wait_recv()

        @pl.when(jnp.logical_and(places[side] > 0, places[side] < last))
        def _():
            pbuf[c, side] = pbuf[c, side] + rbuf[c, side]
            forward(c, side).start()

        @pl.when(places[side] == last)
        def _():
            gate_pre, up_pre, gate_tan = (
                pbuf[c, side, :, pl.ds(i * CHUNK, CHUNK)]
                + rbuf[c, side, :, pl.ds(i * CHUNK, CHUNK)]
                for i in range(3)
            )
            silu_slope, silu_bend = silu_parts(gate_pre)
            scaled = grad[:, where].astype(jnp.float32) * up_pre
            g_ref[c, pl.ds(side * half, half), pl.ds(0, CHUNK)] = (
                scaled * silu_slope
            ).astype(jnp.bfloat16)
            g_ref[c, pl.ds(side * half, half), pl.ds(CHUNK, CHUNK)] = (
                scaled * silu_bend * gate_tan
            ).astype(jnp.bfloat16)
            backward(c, side).start()

    def give_back(s):
        for side in range(2):
            c = s - (2 * last - places[side])
            inside = jnp.logical_and(c >= 0, c < chunks)

            @pl.when(inside)
            def _(c=c, side=side):
                give_back_side(c, side)

    def give_back_side(c, side):
        @pl.when(places[side] < last)
        def _():
            backward(c, side).wait_recv()

        @pl.when(jnp.logical_and(places[side] > 0, places[side] < last))
        def _():
            backward(c, side).start()

    @pl.when(d == 0)
    def _():
        low.wait_recv()

    @pl.when(d == last)
    def _():
        high.wait_recv()

    def step(s, carry):
        @pl.when(s < chunks)
        def _():
            multiply(s)

        relay(s)
        give_back(s)
        return carry

    lax.fori_loop(0, chunks + 2 * last, step, 0)

    def drain(c, carry):
        for side in range(2):

            @pl.when(
                jnp.logical_and(
                    places[side] < last,
                    jnp.logical_or(places[side] > 0, c >= chunks - FLIGHT),
                )
            )
            def _():
                forward(c, side).wait_send()

            @pl.when(places[side] > 0)
            def _():
                backward(c, side).wait_send()

        return carry

    lax.fori_loop(0, chunks, drain, 0)
    for copy in first + second:
        copy.wait_send()

    @pl.when(d == 1)
    def _():
        low.wait_send()

    @pl.when(d == 2)
    def _():
        high.wait_send()


def exchange(padded, grad, gate_weight, up_weight, gate_probe):
    shards, peers = lax.axis_size("dp"), lax.axis_size("mp")
    rows, features = padded.shape
    depth, width = gate_weight.shape
    chunks = width // CHUNK
    total = rows * peers
    half = total // 2
    vmem = pl.BlockSpec(memory_space=pltpu.VMEM)
    hbm = pl.BlockSpec(memory_space=pl.ANY)
    dma = pltpu.SemaphoreType.DMA
    return pl.pallas_call(
        functools.partial(exchange_kernel, shards, peers),
        out_shape=(
            jax.ShapeDtypeStruct((chunks, total, 2 * CHUNK), jnp.bfloat16),
            jax.ShapeDtypeStruct((depth, total), jnp.bfloat16),
        ),
        in_specs=[vmem, vmem, hbm, hbm, hbm],
        out_specs=(vmem, vmem),
        scratch_shapes=[
            pltpu.VMEM((3, depth, width), jnp.bfloat16),
            pltpu.VMEM((shards - 1, rows, depth), jnp.bfloat16),
            pltpu.VMEM((peers, rows, depth), jnp.bfloat16),
            pltpu.VMEM((total, depth), jnp.bfloat16),
            pltpu.VMEM((half, width), jnp.bfloat16),
            pltpu.VMEM((chunks, 2, half, 3 * CHUNK), jnp.float32),
            pltpu.VMEM((chunks, 2, half, 3 * CHUNK), jnp.float32),
            dma((3,)),
            dma((shards - 1,)),
            dma((shards - 1,)),
            dma((peers - 1,)),
            dma((peers - 1,)),
            dma,
            dma,
            dma((chunks, 2)),
            dma((chunks, 2)),
            dma((chunks, 2)),
            dma((chunks, 2)),
        ],
        compiler_params=pltpu.CompilerParams(
            collective_id=0, has_side_effects=True, vmem_limit_bytes=40 << 20
        ),
    )(padded, grad, gate_weight, up_weight, gate_probe)


def update_kernel(
    colt_ref, g_ref, weight_ref, probe_ref, mean_ref, curve_ref, weight_out, mean_out, curve_out
):
    for k in range(GROUPED):
        at = pl.ds(k * CHUNK, CHUNK)
        sums = jnp.dot(colt_ref[...], g_ref[k], preferred_element_type=jnp.float32)
        weight_out[:, at], mean_out[:, at], curve_out[:, at] = adahessian(
            weight_ref[:, at], mean_ref[:, at], curve_ref[:, at],
            sums[:, :CHUNK], probe_ref[:, at], sums[:, CHUNK:],
        )


UPDATE_ROWS = 512


def update(colt, g, weight, probe, mean, curve):
    depth, width = weight.shape
    total = colt.shape[1]
    block = pl.BlockSpec((UPDATE_ROWS, GROUPED * CHUNK), lambda i, j: (j, i))
    return pl.pallas_call(
        update_kernel,
        grid=(width // (GROUPED * CHUNK), depth // UPDATE_ROWS),
        in_specs=[
            pl.BlockSpec((UPDATE_ROWS, total), lambda i, j: (j, 0)),
            pl.BlockSpec((GROUPED, total, 2 * CHUNK), lambda i, j: (i, 0, 0)),
            block, block, block, block,
        ],
        out_specs=(block, block, block),
        out_shape=(
            jax.ShapeDtypeStruct(weight.shape, weight.dtype),
            jax.ShapeDtypeStruct(mean.shape, mean.dtype),
            jax.ShapeDtypeStruct(curve.shape, curve.dtype),
        ),
        compiler_params=pltpu.CompilerParams(vmem_limit_bytes=32 << 20),
    )(colt, g, weight, probe, mean, curve)


def body(
    tokens, hidden_grad, gate_weight, up_weight, gate_probe, gate_mean, gate_curve, group_counts
):
    shards = lax.axis_size("dp")
    local, depth, width = tokens.shape[0], gate_weight.shape[0], gate_weight.shape[1]
    fits = shards == 4 and (shards * local) % 16 == 0 and hidden_grad.shape[0] % 16 == 0
    if not (fits and width % (GROUPED * CHUNK) == 0 and depth % UPDATE_ROWS == 0 and width <= 2048):
        return plain_body(
            tokens, hidden_grad, gate_weight, up_weight, gate_probe,
            gate_mean, gate_curve, group_counts,
        )
    d = lax.axis_index("dp")
    limit = lax.dynamic_index_in_dim(group_counts, d, 0, keepdims=False)
    live = jnp.arange(hidden_grad.shape[0], dtype=jnp.int32) < limit
    grad = jnp.where(live[:, None], hidden_grad, jnp.zeros_like(hidden_grad))
    slot = jnp.arange(shards * local, dtype=jnp.int32) // local
    repeated = jnp.tile(tokens, (shards, 1))
    padded = jnp.where((slot == d)[:, None], repeated, jnp.zeros_like(repeated))
    g, colt = exchange(padded, grad, gate_weight, up_weight, gate_probe)
    return update(colt, g, gate_weight, gate_probe, gate_mean, gate_curve)


def solution(mesh):
    return jax.shard_map(
        body,
        mesh=mesh,
        in_specs=(
            P(("dp", "mp"), None),
            P("dp", "mp"),
            P("dp", "mp"),
            P("dp", "mp"),
            P("dp", "mp"),
            P("dp", "mp"),
            P("dp", "mp"),
            P(),
        ),
        out_specs=(P("dp", "mp"), P("dp", "mp"), P("dp", "mp")),
        check_vma=False,
    )
```
